32 devices in a mesh: seq: 8 (over z, x), rows: 4 (over y, core).
Axes of the slice: x: 2, y: 2, z: 4, core: 2. Of those that a mesh axis runs over, the one named last changes fastest.
Arguments:
- tokens: bfloat16 [2, 4, 1024, 2048], P(None, 'rows', 'seq'), may hold values from -6 to 6
- doc_lengths: int32 [2, 4, 8], P(None, 'rows'), may hold values from 1 to 1017, as said below
- ln1_gain: bfloat16 [2048], P(('seq', 'rows')), may hold values from 0.5 to 1.5
- ln1_bias: bfloat16 [2048], P(('seq', 'rows')), may hold values from -1.75 to 1.75
- w_qkv: bfloat16 [2048, 6144], P(('seq', 'rows')), may hold values from -0.125 to 0.125
- q_bias: bfloat16 [2048], P(('seq', 'rows')), may hold values from -3 to 3
- k_bias_rot: bfloat16 [512], P(('seq', 'rows')), may hold values from -6 to 6
- v_bias: bfloat16 [2048], P(('seq', 'rows')), may hold values from -3 to 3
- w_out: bfloat16 [2048, 2048], P(('seq', 'rows')), may hold values from -0.5 to 0.5
- ln2_gain: bfloat16 [2048], P(('seq', 'rows')), may hold values from 0.5 to 1.5
- ln2_bias: bfloat16 [2048], P(('seq', 'rows')), may hold values from -1.75 to 1.75
- w_gate: bfloat16 [2048, 5632], P(('seq', 'rows')), may hold values from -0.125 to 0.125
- w_up: bfloat16 [2048, 5632], P(('seq', 'rows')), may hold values from -0.125 to 0.125
- w_down: bfloat16 [5632, 2048], P(('seq', 'rows')), may hold values from -0.078125 to 0.078125
- cotangent: bfloat16 [2, 4, 1024, 2048], P(None, 'rows', 'seq'), may hold values from -6 to 6
Outputs:
- output: bfloat16 [2, 4, 1024, 2048], P(None, 'rows', 'seq')
- grad_tokens: bfloat16 [2, 4, 1024, 2048], P(None, 'rows', 'seq')
- grad_ln1_gain: float32 [2048], P(('seq', 'rows'))
- grad_ln1_bias: float32 [2048], P(('seq', 'rows'))
- grad_w_qkv: float32 [2048, 6144], P(('seq', 'rows'))
- grad_q_bias: float32 [2048], P(('seq', 'rows'))
- grad_k_bias_rot: float32 [512], P(('seq', 'rows'))
- grad_v_bias: float32 [2048], P(('seq', 'rows'))
- grad_w_out: float32 [2048, 2048], P(('seq', 'rows'))
- grad_ln2_gain: float32 [2048], P(('seq', 'rows'))
- grad_ln2_bias: float32 [2048], P(('seq', 'rows'))
- grad_w_gate: float32 [2048, 5632], P(('seq', 'rows'))
- grad_w_up: float32 [2048, 5632], P(('seq', 'rows'))
- grad_w_down: float32 [5632, 2048], P(('seq', 'rows'))
The draws below stay inside these ranges and needn't reach their ends.
Inputs may be any that keep to these rules, and one draw needn't show every extreme that they name: `doc_lengths`: the 8 lengths of a row sum to 1024. A row holds either one document of 1017 tokens beside documents of one token, or two documents of about half the row beside short ones of at most 16 tokens; every index of rows has at least one row of the first kind among its micro-batches.
All inputs are finite; a program needn't handle non-finite values.
Results may differ from the reference program's by a relative error of at most 0.023.
Values may be sent and summed in bfloat16 or wider, within the bound.
A program may use at most 576 MiB of HBM per device.

```python
import jax
import jax.numpy as jnp
from jax import lax

D = 2048
HEADS = 32
HD = 64
ROT = 16
FF = 5632
SEQ_TOK = 128
MB = 2
DOCS = 8
ROW_LEN = 1024
ROWS = 4


def draw_doc_lengths(key, part):
    key = jax.random.fold_in(key, 11)
    key_list = jax.random.split(key, 4)
    short_most = SEQ_TOK // DOCS
    small_draw = jax.random.randint(key_list[0], (MB, ROWS, DOCS), 1, short_most + 1)
    big_slot = jax.random.randint(key_list[1], (MB, ROWS, 1), 0, DOCS)
    long_count = jax.random.randint(key_list[2], (1, ROWS, 1), 1, MB + 1)
    shift_by = jax.random.randint(key_list[3], (1, ROWS, 1), 0, MB)
    batch_place = jnp.arange(MB, dtype=jnp.int32)[:, None, None]
    is_long = (batch_place + shift_by) % MB < long_count
    small_len = jnp.where(is_long, 1, small_draw)
    slot_ids = jnp.arange(DOCS, dtype=jnp.int32)[None, None, :]
    partner = (big_slot + DOCS // 2) % DOCS
    first_hit = slot_ids == big_slot
    second_hit = (slot_ids == partner) & jnp.logical_not(is_long)
    keep_small = jnp.logical_not(first_hit | second_hit)
    remain = ROW_LEN - jnp.sum(jnp.where(keep_small, small_len, 0), axis=2, keepdims=True)
    halved = remain // 2
    big_value = jnp.where(is_long, remain, remain - halved)
    return jnp.where(first_hit, big_value, jnp.where(second_hit, halved, small_len)).astype(jnp.int32)


def block_levels(rng, shape, cuts, smallest, top_value):
    def one(axis_at, parts):
        heights = jax.random.uniform(jax.random.fold_in(jax.random.fold_in(rng, 6), axis_at), (parts,), jnp.float32, smallest / len(cuts), top_value / len(cuts))
        return jnp.repeat(jnp.exp(heights), shape[axis_at] // parts).reshape((-1,) + (1,) * (len(shape) - axis_at - 1))

    gain = one(*cuts[0])
    for cut in cuts[1:]:
        gain = gain * one(*cut)
    return gain


def noise(stream_key, extent, spread, bound, cuts=(), kind=jnp.bfloat16):
    values = jax.random.normal(stream_key, extent, jnp.float32) * spread
    if len(cuts) > 0:
        values = block_levels(stream_key, extent, cuts, -0.22, 0.18) * values
    return jnp.clip(values, min=-bound, max=bound).astype(kind)


def setup_inputs(seed: int = 0) -> dict:
    streams_of = jax.random.split(jax.random.key(seed), 16)
    return {
        "tokens": noise(streams_of[0], (MB, ROWS, ROW_LEN, D), 1.0, 6.0, ((1, 4), (2, 8))),
        "doc_lengths": draw_doc_lengths(jax.random.fold_in(streams_of[15], 71), 0),
        "ln1_gain": jnp.clip(1.0 + 0.1 * jax.random.normal(streams_of[2], (D,), jnp.float32), 0.5, 1.5).astype(jnp.bfloat16),
        "ln1_bias": noise(streams_of[3], (D,), 0.3, 1.75, ((0, 32),)),
        "w_qkv": noise(streams_of[4], (D, 3 * D), D ** -0.5, 0.125, ((0, 32),)),
        "q_bias": noise(streams_of[5], (D,), 0.5, 3.0, ((0, 32),)),
        "k_bias_rot": noise(streams_of[6], (HEADS * ROT,), 1.0, 6.0, ((0, 32),)),
        "v_bias": noise(streams_of[7], (D,), 0.5, 3.0, ((0, 32),)),
        "w_out": noise(streams_of[8], (D, D), (D // 16) ** -0.5, 0.5, ((0, 32),)),
        "ln2_gain": jnp.clip(1.0 + 0.1 * jax.random.normal(streams_of[9], (D,), jnp.float32), 0.5, 1.5).astype(jnp.bfloat16),
        "ln2_bias": noise(streams_of[10], (D,), 0.3, 1.75, ((0, 32),)),
        "w_gate": noise(streams_of[11], (D, FF), D ** -0.5, 0.125, ((0, 32),)),
        "w_up": noise(streams_of[12], (D, FF), D ** -0.5, 0.125, ((0, 32),)),
        "w_down": noise(streams_of[13], (FF, D), FF ** -0.5, 0.078125, ((0, 32),)),
        "cotangent": noise(streams_of[14], (MB, ROWS, ROW_LEN, D), 1.0, 6.0, ((1, 4), (2, 8))),
    }


@jax.custom_vjp
def low(v):
    return lax.optimization_barrier(v.astype(jnp.bfloat16)).astype(jnp.float32)

@jax.custom_vjp
def low_back(v):
    return v

def low_keep(v):
    return (low(v), None)

def low_pass(kept, grad):
    return (grad,)

def back_keep(v):
    return (v, None)

def back_low(kept, grad):
    return (low(grad),)
low.defvjp(low_keep, low_pass)
low_back.defvjp(back_keep, back_low)
NORM_EPS = 1e-05
THETA = 10000.0
MASKED = -1e+30
HIGHEST = lax.Precision.HIGHEST

def row_layout(lengths):
    doc_ends = jnp.cumsum(lengths, dtype=jnp.int32)
    places = jnp.arange(ROW_LEN, dtype=jnp.int32)
    passed = (places[:, None] >= doc_ends[None, :]).astype(jnp.int32)
    segment = lax.optimization_barrier(jnp.sum(passed, axis=1, dtype=jnp.int32))
    starts = lax.optimization_barrier(jnp.sum(passed * lengths[None, :], axis=1, dtype=jnp.int32))
    return (segment, places - starts)

def layer_norm(values, norm_gain, norm_bias):
    average = lax.optimization_barrier(jnp.mean(values, axis=-1, keepdims=True))
    centred = values - average
    variance = lax.optimization_barrier(jnp.mean(centred * centred, axis=-1, keepdims=True))
    return centred * lax.rsqrt(variance + NORM_EPS) * norm_gain + norm_bias

def rotary_tables(positions):
    half_rot = ROT // 2
    frequency = THETA ** (-2.0 * jnp.arange(half_rot, dtype=jnp.float32) / ROT)
    angles = positions.astype(jnp.float32)[:, None] * frequency[None, :]
    return (jnp.cos(angles)[:, None, :], jnp.sin(angles)[:, None, :])

def rotate(head_vals, cosine, sine_tab, orient):
    half_rot = ROT // 2
    low_half = head_vals[..., :half_rot]
    high_half = head_vals[..., half_rot:ROT]
    return jnp.concatenate([low_half * cosine - orient * high_half * sine_tab, high_half * cosine + orient * low_half * sine_tab, head_vals[..., ROT:]], axis=-1)

def row_forward(row_in, params, segment, positions):
    norm1_gain, norm1_bias, qkv_weight, query_bias, key_bias_rot, value_bias, out_weight, norm2_gain, norm2_bias, gate_weight, up_weight, down_weight = params
    normed_one = low(layer_norm(row_in, norm1_gain, norm1_bias))
    key_bias = jnp.concatenate([key_bias_rot.reshape(HEADS, ROT), jnp.zeros((HEADS, HD - ROT), jnp.float32)], axis=1).reshape(D)
    bias_all = jnp.concatenate([query_bias, key_bias, value_bias])
    mixed = low_back(jnp.dot(normed_one, qkv_weight, precision=HIGHEST) + bias_all)
    cosine, sine_tab = rotary_tables(positions)
    queries = low(low_back(rotate(mixed[:, :D].reshape(ROW_LEN, HEADS, HD), cosine, sine_tab, 1.0)))
    keys_all = low(low_back(rotate(mixed[:, D:2 * D].reshape(ROW_LEN, HEADS, HD), cosine, sine_tab, 1.0)))
    values_all = low(low_back(mixed[:, 2 * D:].reshape(ROW_LEN, HEADS, HD)))
    places = jnp.arange(ROW_LEN, dtype=jnp.int32)
    allowed = (segment[:, None] == segment[None, :]) & (places[:, None] >= places[None, :])

    def one_head(operands):
        query_head, key_head, value_head = operands
        scores = low_back(jnp.dot(query_head, key_head.T, precision=HIGHEST) * HD ** (-0.5))
        attn_probs = low(jax.nn.softmax(jnp.where(allowed, scores, MASKED), axis=-1))
        return low(low_back(jnp.dot(attn_probs, value_head, precision=HIGHEST)))
    attended = lax.map(jax.checkpoint(one_head), (jnp.swapaxes(queries, 0, 1), jnp.swapaxes(keys_all, 0, 1), jnp.swapaxes(values_all, 0, 1)))
    attended = jnp.swapaxes(attended, 0, 1).reshape(ROW_LEN, D)
    residual = row_in + low_back(jnp.dot(attended, out_weight, precision=HIGHEST))
    normed_two = low(layer_norm(residual, norm2_gain, norm2_bias))
    gate = low_back(jnp.dot(normed_two, gate_weight, precision=HIGHEST))
    up_proj = low_back(jnp.dot(normed_two, up_weight, precision=HIGHEST))
    hidden = low(jax.nn.silu(gate) * up_proj)
    return residual + jnp.dot(hidden, down_weight, precision=HIGHEST)

def reference(tokens, doc_lengths, ln1_gain, ln1_bias, w_qkv, q_bias, k_bias_rot, v_bias, w_out, ln2_gain, ln2_bias, w_gate, w_up, w_down, cotangent):
    params = tuple((weight.astype(jnp.float32) for weight in (ln1_gain, ln1_bias, w_qkv, q_bias, k_bias_rot, v_bias, w_out, ln2_gain, ln2_bias, w_gate, w_up, w_down)))
    row_count = MB * ROWS
    flat_tokens = tokens.reshape(row_count, ROW_LEN, D)
    flat_lengths = doc_lengths.reshape(row_count, DOCS)
    flat_grads = cotangent.reshape(row_count, ROW_LEN, D)
    start_sums = jax.tree.map(jnp.zeros_like, params)

    def one_row(summed, row_data):
        row_in, lengths, row_grad = row_data
        segment, positions = row_layout(lengths)

        def forward(values, weights):
            return row_forward(values, weights, segment, positions)
        result, pullback = jax.vjp(forward, row_in.astype(jnp.float32), params)
        grad_in, grad_params = pullback(row_grad.astype(jnp.float32))
        summed = jax.tree.map(jnp.add, summed, grad_params)
        return (summed, (result.astype(jnp.bfloat16), grad_in.astype(jnp.bfloat16)))
    summed, (outputs, grads_in) = lax.scan(one_row, start_sums, (flat_tokens, flat_lengths, flat_grads))
    return (outputs.reshape(MB, ROWS, ROW_LEN, D), grads_in.reshape(MB, ROWS, ROW_LEN, D), summed[0], summed[1], summed[2], summed[3], summed[4], summed[5], summed[6], summed[7], summed[8], summed[9], summed[10], summed[11])
```

```python
import jax
import jax.numpy as jnp
from jax import lax
from jax.experimental import pallas as pl
from jax.experimental.pallas import tpu as pltpu
from jax.sharding import Mesh, PartitionSpec as P

D = 2048
HEADS = 32
HD = 64
ROT = 16
FF = 5632
MB = 2
Z = 4

NORM_EPS = 1e-05
THETA = 10000.0
MASKED = -1e30

ALL = ("z", "x", "y", "core")
PLANE = ("x", "y", "core")
TOKENS = ("y", "core", "x")


def dot_last(left, right):
    return lax.dot_general(
        left, right, (((1,), (1,)), ((), ())), preferred_element_type=jnp.float32
    )


def dot_first(left, right):
    return lax.dot_general(
        left, right, (((0,), (0,)), ((), ())), preferred_element_type=jnp.float32
    )


def dot(left, right):
    return jnp.dot(left, right, preferred_element_type=jnp.float32)


def row_layout(lengths, row_len):
    doc_ends = jnp.cumsum(lengths, dtype=jnp.int32)
    places = jnp.arange(row_len, dtype=jnp.int32)
    passed = (places[:, None] >= doc_ends[None, :]).astype(jnp.int32)
    segment = jnp.sum(passed, axis=1, dtype=jnp.int32)
    starts = jnp.sum(passed * lengths[None, :], axis=1, dtype=jnp.int32)
    return (segment, places - starts)


def norm_forward(values, norm_gain, norm_bias):
    average = jnp.mean(values, axis=-1, keepdims=True)
    centred = values - average
    inv_dev = lax.rsqrt(jnp.mean(centred * centred, axis=-1, keepdims=True) + NORM_EPS)
    scaled = centred * inv_dev
    return (scaled * norm_gain + norm_bias, scaled, inv_dev)


def norm_backward(grad_normed, scaled, inv_dev, norm_gain):
    grad_scaled = grad_normed * norm_gain
    first_mean = jnp.mean(grad_scaled, axis=-1, keepdims=True)
    second_mean = jnp.mean(grad_scaled * scaled, axis=-1, keepdims=True)
    return inv_dev * (grad_scaled - first_mean - scaled * second_mean)


def rotary_tables(positions):
    half_rot = ROT // 2
    frequency = THETA ** (-2.0 * jnp.arange(half_rot, dtype=jnp.float32) / ROT)
    angles = positions.astype(jnp.float32)[:, None] * frequency[None, :]
    return (jnp.cos(angles)[:, None, :], jnp.sin(angles)[:, None, :])


def rotate(head_vals, cosine, sine_tab, orient):
    half_rot = ROT // 2
    low_half = head_vals[..., :half_rot]
    high_half = head_vals[..., half_rot:ROT]
    return jnp.concatenate(
        [
            low_half * cosine - orient * high_half * sine_tab,
            high_half * cosine + orient * low_half * sine_tab,
            head_vals[..., ROT:],
        ],
        axis=-1,
    )


def masked_scores(queries, keys, segment):
    places = jnp.arange(segment.shape[0], dtype=jnp.int32)
    allowed = (segment[:, None] == segment[None, :]) & (places[:, None] >= places[None, :])
    scores = jnp.einsum(
        "qhd,khd->hqk", queries, keys, preferred_element_type=jnp.float32
    ) * HD ** (-0.5)
    return jnp.where(allowed[None], scores, MASKED)


def attend_forward(queries, keys, values, segment):
    scores = masked_scores(queries, keys, segment)
    row_peak = jnp.max(scores, axis=-1, keepdims=True)
    raised = jnp.exp(scores - row_peak)
    totals = jnp.sum(raised, axis=-1, keepdims=True)
    probs_low = (raised / totals).astype(jnp.bfloat16)
    attended = jnp.einsum("hqk,khd->qhd", probs_low, values, preferred_element_type=jnp.float32)
    return (attended.astype(jnp.bfloat16), row_peak + jnp.log(totals))


def attend_backward(queries, keys, values, segment, log_totals, grad):
    scale = HD ** (-0.5)
    scores = masked_scores(queries, keys, segment)
    attn_probs = jnp.exp(scores - log_totals)
    grad_probs = jnp.einsum("qhd,khd->hqk", grad, values, preferred_element_type=jnp.float32)
    inner_sum = jnp.sum(attn_probs * grad_probs, axis=-1, keepdims=True)
    grad_scores = (attn_probs * (grad_probs - inner_sum)).astype(jnp.bfloat16)
    grad_q = jnp.einsum("hqk,khd->qhd", grad_scores, keys, preferred_element_type=jnp.float32)
    grad_k = jnp.einsum("hqk,qhd->khd", grad_scores, queries, preferred_element_type=jnp.float32)
    grad_v = jnp.einsum(
        "hqk,qhd->khd", attn_probs.astype(jnp.bfloat16), grad, preferred_element_type=jnp.float32
    )
    return (
        (grad_q * scale).astype(jnp.bfloat16).astype(jnp.float32),
        (grad_k * scale).astype(jnp.bfloat16).astype(jnp.float32),
        grad_v,
    )


def local(
    tokens,
    doc_lengths,
    ln1_gain,
    ln1_bias,
    w_qkv,
    q_bias,
    k_bias_rot,
    v_bias,
    w_out,
    ln2_gain,
    ln2_bias,
    w_gate,
    w_up,
    w_down,
    cotangent,
):
    xs, ys, cs = (lax.axis_size(name) for name in PLANE)
    z_at, x_at, y_at, c_at = (lax.axis_index(name) for name in ALL)
    plane = xs * ys * cs
    count = Z * plane
    rank = (x_at * ys + y_at) * cs + c_at
    local_len = tokens.shape[2]
    row_len = local_len * Z * xs
    rows_here = ys * cs // Z
    block = D // count
    rot_block = HEADS * ROT // count
    ff_block = FF // count
    heads_here = HEADS // plane
    strided = block == HD
    width = heads_here * HD
    ff_here = Z * ff_block

    there, back = [], []
    for z in range(Z):
        for x in range(xs):
            for r in range(ys * cs):
                source = (z * xs + x) * ys * cs + r
                target = ((r // rows_here) * xs + x) * ys * cs + (r % rows_here) * Z + z
                there.append((source, target))
                back.append((target, source))

    pieces = [ln1_gain, ln1_bias, q_bias, v_bias, ln2_gain, ln2_bias, k_bias_rot]
    packed = jnp.concatenate(
        [piece.astype(jnp.float32) for piece in pieces]
        + [doc_lengths[:, 0].astype(jnp.float32).reshape(-1)]
    )
    pack_len = -(-packed.shape[0] // 512) * 512
    packed = jnp.pad(packed, (0, pack_len - packed.shape[0])).reshape(1, -1, 128)
    small = lax.all_gather(packed, ALL, axis=0, tiled=True).reshape(count, pack_len)
    fulls = [small[:, i * block : (i + 1) * block].reshape(D) for i in range(6)]
    norm1_gain, norm1_bias, q_full, v_full, norm2_gain, norm2_bias = fulls
    k_rot = small[:, 6 * block : 6 * block + rot_block].reshape(HEADS, ROT)
    k_full = jnp.concatenate([k_rot, jnp.zeros((HEADS, HD - ROT), jnp.float32)], axis=1)
    at = 6 * block + rot_block
    lengths_all = small[: ys * cs, at : at + MB * 8].reshape(ys * cs, MB, 8).astype(jnp.int32)
    lengths = lax.dynamic_slice_in_dim(lengths_all, z_at * rows_here, rows_here, 0)

    def my_heads(full):
        if strided:
            by_rank = full.reshape(heads_here, plane, HD)
            return lax.dynamic_index_in_dim(by_rank, rank, 1, False).reshape(width)
        by_rank = full.reshape(plane, width)
        return lax.dynamic_index_in_dim(by_rank, rank, 0, False)

    bias_here = jnp.concatenate([my_heads(q_full), my_heads(k_full), my_heads(v_full)])

    if strided:
        cut_qkv = w_qkv.reshape(block, 3, heads_here, plane, HD).transpose(3, 0, 1, 2, 4)
    else:
        cut_qkv = w_qkv.reshape(block, 3, plane, heads_here, HD).transpose(2, 0, 1, 3, 4)
    cut_qkv = cut_qkv.reshape(plane, block, 3 * width)

    def cut_ff(weight):
        cut = weight.reshape(block, Z, plane, ff_block).transpose(2, 0, 1, 3)
        return cut.reshape(plane, block, ff_here)

    cut_gu = jnp.concatenate([cut_ff(w_gate), cut_ff(w_up)], axis=2)
    here_qkv = lax.all_to_all(cut_qkv, PLANE, 0, 0, tiled=True).reshape(plane * block, 3 * width)
    here_gu = lax.all_to_all(cut_gu, PLANE, 0, 0, tiled=True).reshape(plane * block, 2 * ff_here)
    col_qkv = lax.all_gather(here_qkv, "z", axis=0, tiled=True)
    if strided:
        row_out = lax.all_gather(w_out, "z", axis=0, tiled=True)
    else:
        row_out = lax.dynamic_slice_in_dim(
            lax.all_gather(w_out, ALL, axis=0, tiled=True), rank * width, width, 0
        )
    col_gu = lax.all_gather(here_gu, "z", axis=0, tiled=True)
    row_down = lax.all_gather(w_down, "z", axis=0, tiled=True)

    tokens_here = lax.ppermute(tokens[:, 0], ALL, there)
    cot_here = lax.ppermute(cotangent[:, 0], ALL, there)

    def gather(chunk):
        return lax.all_gather(chunk, TOKENS, axis=0, tiled=True)

    def scatter(partial):
        return lax.psum_scatter(
            partial.astype(jnp.bfloat16), TOKENS, scatter_dimension=0, tiled=True
        ).astype(jnp.float32)

    outputs, grads_in, kept = [], [], []
    small_sums = None
    for m in range(MB):
        layouts = [row_layout(lengths[row, m], row_len) for row in range(rows_here)]
        tables = [rotary_tables(positions) for _, positions in layouts]
        chunk = tokens_here[m].astype(jnp.float32)
        normed_one, scaled_one, inv_one = norm_forward(chunk, norm1_gain, norm1_bias)
        all_one = gather(normed_one.astype(jnp.bfloat16))
        all_cot = gather(cot_here[m])
        mixed = (dot(all_one, col_qkv) + bias_here).reshape(
            rows_here, row_len, 3, heads_here, HD
        )
        heads, attended = [], []
        for row in range(rows_here):
            cosine, sine_tab = tables[row]
            queries = rotate(mixed[row, :, 0], cosine, sine_tab, 1.0).astype(jnp.bfloat16)
            keys = rotate(mixed[row, :, 1], cosine, sine_tab, 1.0).astype(jnp.bfloat16)
            values = mixed[row, :, 2].astype(jnp.bfloat16)
            segment = layouts[row][0]
            result, log_totals = attend_forward(queries, keys, values, segment)
            heads.append((queries, keys, values, segment, log_totals))
            attended.append(result.reshape(row_len, width))
        attended = jnp.concatenate(attended, axis=0)
        residual = chunk + scatter(dot(attended, row_out))
        normed_two, scaled_two, inv_two = norm_forward(residual, norm2_gain, norm2_bias)
        all_two = gather(normed_two.astype(jnp.bfloat16))
        gate_up = dot(all_two, col_gu)
        gate, up_proj = gate_up[:, :ff_here], gate_up[:, ff_here:]
        sigmoid_gate = jax.nn.sigmoid(gate)
        silu_gate = gate * sigmoid_gate
        hidden = (silu_gate * up_proj).astype(jnp.bfloat16)
        outputs.append((residual + scatter(dot(hidden, row_down))).astype(jnp.bfloat16))
        grad_hidden = dot_last(all_cot, row_down)
        grad_gate = grad_hidden * up_proj * sigmoid_gate * (1.0 + gate * (1.0 - sigmoid_gate))
        grad_gu = jnp.concatenate(
            [grad_gate.astype(jnp.bfloat16), (grad_hidden * silu_gate).astype(jnp.bfloat16)],
            axis=1,
        )
        grad_two = scatter(dot_last(grad_gu, col_gu))
        grad_residual = cot_here[m].astype(jnp.float32) + norm_backward(
            grad_two, scaled_two, inv_two, norm2_gain
        )
        all_branch = gather(grad_residual.astype(jnp.bfloat16))
        grad_attended = dot_last(all_branch, row_out).astype(jnp.bfloat16)
        grad_attended = grad_attended.reshape(rows_here, row_len, heads_here, HD)
        grad_mixed = []
        for row in range(rows_here):
            cosine, sine_tab = tables[row]
            grad_q, grad_k, grad_v = attend_backward(*heads[row], grad_attended[row])
            grad_q = rotate(grad_q, cosine, sine_tab, -1.0)
            grad_k = rotate(grad_k, cosine, sine_tab, -1.0)
            stacked = jnp.stack([grad_q, grad_k, grad_v], axis=1).astype(jnp.bfloat16)
            grad_mixed.append(stacked.reshape(row_len, 3 * width))
        grad_mixed = jnp.concatenate(grad_mixed, axis=0)
        grad_one = scatter(dot_last(grad_mixed, col_qkv))
        grads_in.append(
            (grad_residual + norm_backward(grad_one, scaled_one, inv_one, norm1_gain)).astype(
                jnp.bfloat16
            )
        )
        sums = [
            jnp.sum(grad_one * scaled_one, axis=0),
            jnp.sum(grad_one, axis=0),
            jnp.sum(grad_two * scaled_two, axis=0),
            jnp.sum(grad_two, axis=0),
            jnp.sum(grad_mixed.astype(jnp.float32), axis=0),
        ]
        small_sums = sums if m == 0 else [a + b for a, b in zip(small_sums, sums)]
        kept.append((all_one, grad_mixed, attended, all_branch, all_two, grad_gu, hidden, all_cot))

    joined = [jnp.concatenate(parts, axis=0) for parts in zip(*kept)]

    def over_z(term):
        return lax.psum_scatter(
            term.astype(jnp.bfloat16), "z", scatter_dimension=0, tiled=True
        )

    share_down = over_z(dot_first(joined[6], joined[7])).astype(jnp.float32)
    share_gu = over_z(dot_first(joined[4], joined[5])).reshape(plane, block, 2 * ff_here)
    grad_out = dot_first(joined[2], joined[3])
    if strided:
        share_out = over_z(grad_out).astype(jnp.float32)
    else:
        placed = lax.dynamic_update_slice_in_dim(
            jnp.zeros((D, D), jnp.float32), grad_out, rank * width, 0
        )
        share_out = lax.psum_scatter(
            placed.astype(jnp.bfloat16), ALL, scatter_dimension=0, tiled=True
        ).astype(jnp.float32)
    share_qkv = over_z(dot_first(joined[0], joined[1])).reshape(plane, block, 3 * width)
    share_gu = lax.all_to_all(share_gu, PLANE, 0, 0, tiled=True).astype(jnp.float32)
    share_qkv = lax.all_to_all(share_qkv, PLANE, 0, 0, tiled=True).astype(jnp.float32)

    def join_ff(part):
        return part.reshape(plane, block, Z, ff_block).transpose(1, 2, 0, 3).reshape(block, FF)

    share_gate = join_ff(share_gu[:, :, :ff_here])
    share_up = join_ff(share_gu[:, :, ff_here:])
    if strided:
        share_qkv = share_qkv.reshape(plane, block, 3, heads_here, HD).transpose(1, 2, 3, 0, 4)
    else:
        share_qkv = share_qkv.reshape(plane, block, 3, heads_here, HD).transpose(1, 2, 0, 3, 4)
    share_qkv = share_qkv.reshape(block, 3 * D)

    mine = (jnp.arange(plane) == rank).astype(jnp.float32)

    def spread(part):
        if strided:
            whole = part.reshape(heads_here, 1, HD) * mine[None, :, None]
        else:
            whole = part.reshape(1, heads_here, HD) * mine[:, None, None]
        return whole.reshape(HEADS, HD)

    mixed_sums = small_sums[4].reshape(3, width)
    k_sums = spread(mixed_sums[1])[:, :ROT]
    terms = [
        small_sums[0].reshape(count, block),
        small_sums[1].reshape(count, block),
        spread(mixed_sums[0]).reshape(count, block),
        spread(mixed_sums[2]).reshape(count, block),
        small_sums[2].reshape(count, block),
        small_sums[3].reshape(count, block),
        k_sums.reshape(count, rot_block),
    ]
    packed = jnp.concatenate(terms, axis=1)
    packed = jnp.pad(packed, ((0, 0), (0, pack_len - packed.shape[1])))
    shares = lax.psum_scatter(
        packed.reshape(count, -1, 128), ALL, scatter_dimension=0, tiled=True
    ).reshape(pack_len)
    small_shares = [shares[i * block : (i + 1) * block] for i in range(6)]
    share_k = shares[6 * block : 6 * block + rot_block]

    output = lax.ppermute(jnp.stack(outputs), ALL, back)[:, None]
    grad_tokens = lax.ppermute(jnp.stack(grads_in), ALL, back)[:, None]
    return (
        output,
        grad_tokens,
        small_shares[0],
        small_shares[1],
        share_qkv,
        small_shares[2],
        share_k,
        small_shares[3],
        share_out,
        small_shares[4],
        small_shares[5],
        share_gate,
        share_up,
        share_down,
    )


TOK = 128
N_TOK = 8
VMEM_BYTES = 56 * 2**20
ANY_SPEC = pl.BlockSpec(memory_space=pl.ANY)
VMEM_SPEC = pl.BlockSpec(memory_space=pltpu.VMEM)
DMA = pltpu.SemaphoreType.DMA


def remote(src, dst, sends, recvs, index, device):
    return pltpu.make_async_remote_copy(
        src_ref=src,
        dst_ref=dst,
        send_sem=sends.at[index],
        recv_sem=recvs.at[index],
        device_id=device,
        device_id_type=pl.DeviceIdType.MESH,
    )


class Place:
    def __init__(self):
        self.z, self.x, self.y, self.c = (lax.axis_index(name) for name in ALL)
        self.ox, self.oy, self.oc = 1 - self.x, 1 - self.y, 1 - self.c
        self.px = (self.z, self.ox, self.y, self.c)
        self.py = (self.z, self.x, self.oy, self.c)
        self.ps = (self.z, self.x, self.y, self.oc)
        self.rank = (self.x * 2 + self.y) * 2 + self.c

        self.partners = [(2 * self.c + j, self.x, self.y, self.z // 2) for j in range(2)]
        self.apart = [self.z != 2 * self.c + j for j in range(2)]


def greet(devices, place=None):
    barrier = pltpu.get_barrier_semaphore()
    for device in devices:
        pl.semaphore_signal(
            barrier, inc=1, device_id=device, device_id_type=pl.DeviceIdType.MESH
        )
    extra = 0
    if place is not None:
        for j in range(2):
            extra = extra + lax.select(place.apart[j], 1, 0)

            @pl.when(place.apart[j])
            def _():
                pl.semaphore_signal(
                    barrier,
                    inc=1,
                    device_id=place.partners[j],
                    device_id_type=pl.DeviceIdType.MESH,
                )

    pl.semaphore_wait(barrier, len(devices) + extra)


def hop(src, dst, send, recv, device):
    return pltpu.make_async_remote_copy(
        src_ref=src,
        dst_ref=dst,
        send_sem=send,
        recv_sem=recv,
        device_id=device,
        device_id_type=pl.DeviceIdType.MESH,
    )


def hop_start(apart, src, dst, send, recv, device):
    @pl.when(apart)
    def _():
        hop(src, dst, send, recv, device).start()

    @pl.when(jnp.logical_not(apart))
    def _():
        pltpu.make_async_copy(src, dst, recv).start()


def hop_landed(apart, spot, send, recv, device):
    @pl.when(apart)
    def _():
        hop(spot, spot, send, recv, device).wait_recv()

    @pl.when(jnp.logical_not(apart))
    def _():
        pltpu.make_async_copy(spot, spot, recv).wait()


def hop_sent(apart, src, send, recv, device):
    @pl.when(apart)
    def _():
        hop(src, src, send, recv, device).wait_send()


class MoveIn:
    def __init__(self, place, src, out, swap, sends, recvs):
        self.place, self.src, self.out, self.swap = place, src, out, swap
        self.sends, self.recvs = sends, recvs
        z, x, y, c = place.z, place.x, place.y, place.c
        self.slot = z % 2
        self.mine = (2 * c + y, x, y, z // 2)
        self.other = (2 * c + 1 - y, x, y, z // 2)
        self.mine_apart = z != 2 * c + y
        self.other_apart = z != 2 * c + 1 - y

    def start(self):
        y, recv = self.place.y, self.recvs.at[self.slot]
        across = self.src.at[1 - y]
        hop(across, self.swap, self.sends.at[2], self.recvs.at[2], self.place.py).start()
        hop_start(
            self.mine_apart, self.src.at[y], self.out.at[self.slot], self.sends.at[0], recv, self.mine
        )

    def middle(self):
        recv = self.recvs.at[self.slot]
        hop(self.swap, self.swap, self.sends.at[2], self.recvs.at[2], self.place.py).wait_recv()
        hop_start(
            self.other_apart, self.swap, self.out.at[self.slot], self.sends.at[1], recv, self.other
        )

    def finish(self):
        place, recv = self.place, self.recvs.at[self.slot]
        for j in range(2):
            hop_landed(
                place.apart[j], self.out.at[j], self.sends.at[j], self.recvs.at[j], place.partners[j]
            )
        hop_sent(self.mine_apart, self.src.at[place.y], self.sends.at[0], recv, self.mine)
        hop_sent(self.other_apart, self.swap, self.sends.at[1], recv, self.other)
        hop(self.swap, self.swap, self.sends.at[2], self.recvs.at[2], place.py).wait_send()


class MoveBack:
    def __init__(self, place, own, out, swap, sends, recvs):
        self.place, self.own, self.out, self.swap = place, own, out, swap
        self.sends, self.recvs = sends, recvs
        self.slot = place.z % 2

    def half(self, h):
        return pl.ds(h * (TOK // 2), TOK // 2)

    def start(self):
        place = self.place
        for h in range(2):
            rows = self.half(h)
            recv = self.recvs.at[2 * self.slot + h]
            for j in range(2):
                for straight in (True, False):
                    dst = self.out.at[place.y, rows] if straight else self.swap.at[rows]

                    @pl.when((place.y == self.slot) == straight)
                    def _():
                        hop_start(
                            place.apart[j],
                            self.own.at[j, rows],
                            dst,
                            self.sends.at[2 * j + h],
                            recv,
                            place.partners[j],
                        )

    def landed(self, index, h, spot):
        place = self.place
        device = (2 * place.c + index, place.x, place.y, place.z // 2)
        apart = place.z != 2 * place.c + index
        hop_landed(apart, spot, self.sends.at[h], self.recvs.at[2 * index + h], device)

    def middle(self):
        place = self.place
        for h in range(2):
            rows = self.half(h)
            self.landed(1 - place.y, h, self.swap.at[rows])
            hop(
                self.swap.at[rows],
                self.out.at[place.y, rows],
                self.sends.at[4 + h],
                self.recvs.at[4 + h],
                place.py,
            ).start()

    def finish(self):
        place = self.place
        for h in range(2):
            rows = self.half(h)
            self.landed(place.y, h, self.out.at[place.y, rows])
            spot = self.out.at[1 - place.y, rows]
            hop(spot, spot, self.sends.at[4 + h], self.recvs.at[4 + h], place.py).wait_recv()
            for j in range(2):
                hop_sent(
                    place.apart[j],
                    self.own.at[j, rows],
                    self.sends.at[2 * j + h],
                    self.recvs.at[2 * self.slot + h],
                    place.partners[j],
                )
            hop(
                self.swap.at[rows],
                self.swap.at[rows],
                self.sends.at[4 + h],
                self.recvs.at[4 + h],
                place.py,
            ).wait_send()


MOVE_SCRATCH = [pltpu.VMEM((TOK, D), jnp.bfloat16), DMA((6,)), DMA((6,))]
WHOLE = (2, 2, 2, 2, TOK)


class Gather:
    def __init__(self, place, own, out, sends, recvs):
        self.place, self.own, self.out = place, own, out
        self.sends, self.recvs = sends, recvs
        x, y, ox, oy = place.x, place.y, place.ox, place.oy
        self.me, self.by_x, self.by_y, self.far = (x, y), (ox, y), (x, oy), (ox, oy)
        self.started, self.keep = [], []

    def spot(self, j, chip, core):
        return self.out.at[chip[1], core, j, chip[0]]

    def go(self, src, j, chip, index, device):
        dst = self.spot(j, chip, self.place.c)
        copy = remote(src, dst, self.sends, self.recvs, index, device)
        copy.start()
        self.started.append(copy)

    def landed(self, j, chip, index, device, core=None):
        spot = self.spot(j, chip, self.place.c if core is None else core)
        remote(spot, spot, self.sends, self.recvs, index, device).wait_recv()
        return spot

    def send(self, j):
        place, own, me = self.place, self.own.at[j], self.me
        if j == 0:
            self.go(own, 0, me, 0, place.px)
            self.go(own, 0, me, 3, place.py)
        else:
            self.go(own, 1, me, 1, place.py)
            self.go(own, 1, me, 2, place.px)
        self.go(own, j, me, 6 + j, place.ps)
        copy = pltpu.make_async_copy(own, self.spot(j, me, place.c), self.sends.at[14 + j])
        copy.start()
        self.keep.append(copy)

    def relay(self):
        place = self.place
        spot = self.landed(0, self.by_x, 0, place.px)
        self.go(spot, 0, self.by_x, 5, place.py)
        self.go(spot, 0, self.by_x, 9, place.ps)
        spot = self.landed(1, self.by_y, 1, place.py)
        self.go(spot, 1, self.by_y, 4, place.px)
        self.go(spot, 1, self.by_y, 8, place.ps)

    def hand_over(self):
        place = self.place
        spot = self.landed(0, self.by_y, 3, place.py)
        self.go(spot, 0, self.by_y, 11, place.ps)
        spot = self.landed(1, self.by_x, 2, place.px)
        self.go(spot, 1, self.by_x, 10, place.ps)

    def hand_over_far(self):
        place = self.place
        spot = self.landed(0, self.far, 5, place.py)
        self.go(spot, 0, self.far, 13, place.ps)
        spot = self.landed(1, self.far, 4, place.px)
        self.go(spot, 1, self.far, 12, place.ps)

    def finish(self):
        for j, chip, index in (
            (0, self.me, 6),
            (1, self.me, 7),
            (1, self.by_y, 8),
            (0, self.by_x, 9),
            (1, self.by_x, 10),
            (0, self.by_y, 11),
            (1, self.far, 12),
            (0, self.far, 13),
        ):
            self.landed(j, chip, index, self.place.ps, self.place.oc)
        for copy in self.keep:
            copy.wait()
        for copy in self.started:
            copy.wait_send()

    def steps(self):
        self.send(0)
        self.send(1)
        yield
        self.relay()
        yield
        self.hand_over()
        yield
        self.hand_over_far()
        yield
        self.finish()


GATHER_SEMS = 16
SUM_SEMS = 10
SUM_SCRATCH = [
    pltpu.VMEM((4, 2, TOK, D), jnp.bfloat16),
    pltpu.VMEM((4, 2, TOK, D), jnp.bfloat16),
    pltpu.VMEM((4, 2, TOK, D), jnp.float32),
    pltpu.VMEM((2, TOK, D), jnp.bfloat16),
    pltpu.VMEM((6, TOK, D), jnp.bfloat16),
    pltpu.VMEM((4, TOK, D), jnp.bfloat16),
    DMA((SUM_SEMS,)),
    DMA((SUM_SEMS,)),
]
COLUMNS = 512


def plane_sum(place, acts, weight, turned, scratch, finish, idle=None):
    to_sib, from_sib, mine, through, onward, final, sends, recvs = scratch
    x, y, c = place.x, place.y, place.c

    def times(tx, ty, core, store):
        left = acts[ty, core, :, tx].reshape(2 * TOK, acts.shape[-1])

        def tile(j, _):
            cols = pl.ds(pl.multiple_of(j * COLUMNS, COLUMNS), COLUMNS)
            if turned:
                result = dot_last(left, weight[cols, :])
            else:
                result = dot(left, weight[:, cols])
            store(cols, result.reshape(2, TOK, COLUMNS))
            return 0

        lax.fori_loop(0, D // COLUMNS, tile, 0)

    places = ((place.ox, place.oy), (place.ox, y), (x, place.oy), (x, y))

    def products(q):
        tx, ty = places[q]

        def keep_out(cols, result):
            to_sib[q, :, :, cols] = result.astype(jnp.bfloat16)

        def keep_in(cols, result):
            mine[q, :, :, cols] = result

        times(tx, ty, place.oc, keep_out)
        copy = remote(to_sib.at[q], from_sib.at[q], sends, recvs, q, place.ps)
        copy.start()
        times(tx, ty, c, keep_in)
        copy.wait()

    def chip(q, m):
        return mine[q, m] + from_sib[q, m].astype(jnp.float32)

    def go(src, dst, index, device):
        copy = remote(src, dst, sends, recvs, index, device)
        copy.start()
        return copy

    def landed(spot, index, device):
        remote(spot, spot, sends, recvs, index, device).wait_recv()

    started = []
    products(0)
    onward[0] = chip(0, 0).astype(jnp.bfloat16)
    started.append(go(onward.at[0], through.at[0], 4, place.px))
    onward[1] = chip(0, 1).astype(jnp.bfloat16)
    started.append(go(onward.at[1], through.at[1], 5, place.py))
    products(1)
    onward[2] = chip(1, 0).astype(jnp.bfloat16)
    started.append(go(onward.at[2], final.at[0], 6, place.px))
    products(2)
    landed(through.at[0], 4, place.px)
    onward[5] = (chip(2, 0) + through[0].astype(jnp.float32)).astype(jnp.bfloat16)
    started.append(go(onward.at[5], final.at[2], 9, place.py))
    onward[3] = chip(2, 1).astype(jnp.bfloat16)
    started.append(go(onward.at[3], final.at[3], 7, place.py))
    landed(through.at[1], 5, place.py)
    onward[4] = (chip(1, 1) + through[1].astype(jnp.float32)).astype(jnp.bfloat16)
    started.append(go(onward.at[4], final.at[1], 8, place.px))
    products(3)
    if idle is not None:
        idle()

    def total(m):
        return chip(3, m) + final[m].astype(jnp.float32) + final[2 + m].astype(jnp.float32)

    landed(final.at[0], 6, place.px)
    landed(final.at[2], 9, place.py)
    finish(0, total(0))
    if idle is not None:
        idle()
    landed(final.at[1], 8, place.px)
    landed(final.at[3], 7, place.py)
    finish(1, total(1))
    for copy in started:
        copy.wait_send()


def sum_steps(place, parts, result, scratch):
    from_sib, mine, through, onward, final, sends, recvs, loads = scratch
    x, y, c = place.x, place.y, place.c
    places = ((place.ox, place.oy), (place.ox, y), (x, place.oy), (x, y))
    to_sib, local = [], []
    for q, (tx, ty) in enumerate(places):
        source = parts.at[ty, place.oc, :, tx]
        copy = remote(source, from_sib.at[q], sends, recvs, q, place.ps)
        copy.start()
        to_sib.append(copy)
        copy = pltpu.make_async_copy(parts.at[ty, c, :, tx], mine.at[q], loads.at[q])
        copy.start()
        local.append(copy)

    def chip(q, m):
        return mine[q, m].astype(jnp.float32) + from_sib[q, m].astype(jnp.float32)

    def sib_landed(q):
        to_sib[q].wait()
        local[q].wait()

    def go(src, dst, index, device):
        copy = remote(src, dst, sends, recvs, index, device)
        copy.start()
        return copy

    def landed(spot, index, device):
        remote(spot, spot, sends, recvs, index, device).wait_recv()

    started = []
    yield
    sib_landed(0)
    onward[0] = chip(0, 0).astype(jnp.bfloat16)
    started.append(go(onward.at[0], through.at[0], 4, place.px))
    onward[1] = chip(0, 1).astype(jnp.bfloat16)
    started.append(go(onward.at[1], through.at[1], 5, place.py))
    sib_landed(1)
    onward[2] = chip(1, 0).astype(jnp.bfloat16)
    started.append(go(onward.at[2], final.at[0], 6, place.px))
    sib_landed(2)
    onward[3] = chip(2, 1).astype(jnp.bfloat16)
    started.append(go(onward.at[3], final.at[3], 7, place.py))
    yield
    landed(through.at[1], 5, place.py)
    onward[4] = (chip(1, 1) + through[1].astype(jnp.float32)).astype(jnp.bfloat16)
    started.append(go(onward.at[4], final.at[1], 8, place.px))
    landed(through.at[0], 4, place.px)
    onward[5] = (chip(2, 0) + through[0].astype(jnp.float32)).astype(jnp.bfloat16)
    started.append(go(onward.at[5], final.at[2], 9, place.py))
    sib_landed(3)
    yield
    landed(final.at[0], 6, place.px)
    landed(final.at[3], 7, place.py)
    landed(final.at[1], 8, place.px)
    landed(final.at[2], 9, place.py)
    for copy in started:
        copy.wait_send()
    for m in range(2):
        result(
            m, chip(3, m) + final[m].astype(jnp.float32) + final[2 + m].astype(jnp.float32)
        )


STEP_SCRATCH = [
    pltpu.VMEM((4, 2, TOK, D), jnp.bfloat16),
    pltpu.VMEM((4, 2, TOK, D), jnp.bfloat16),
    pltpu.VMEM((2, TOK, D), jnp.bfloat16),
    pltpu.VMEM((6, TOK, D), jnp.bfloat16),
    pltpu.VMEM((4, TOK, D), jnp.bfloat16),
    DMA((SUM_SEMS,)),
    DMA((SUM_SEMS,)),
    DMA((4,)),
]


def kernel_call(body, out_shape, out_specs, in_specs, scratch, ident, args):
    return pl.pallas_call(
        body,
        out_shape=out_shape,
        in_specs=in_specs,
        out_specs=out_specs,
        scratch_shapes=scratch,
        compiler_params=pltpu.CompilerParams(
            collective_id=ident, has_side_effects=True, vmem_limit_bytes=VMEM_BYTES
        ),
    )(*args)


def shape(dims, kind=jnp.bfloat16):
    return jax.ShapeDtypeStruct(dims, kind)


def plane_peers(place):
    peers = []
    for k in range(1, 8):
        dx, dy, dc = k // 4, k // 2 % 2, k % 2
        px, py, pc = (place.x + dx) % 2, (place.y + dy) % 2, (place.c + dc) % 2
        peers.append(((place.z, px, py, pc), (px * 2 + py) * 2 + pc))
    return peers


def z_peers(place):
    return [((place.z + j) % Z, place.x, place.y, place.c) for j in range(1, Z)]


def exchange_start(place, src, dst, sends, recvs, base):
    me = place.rank
    own = pltpu.make_async_copy(src.at[me], dst.at[me], sends.at[base])
    own.start()
    started = []
    for k, (device, rank) in enumerate(plane_peers(place)):
        copy = remote(src.at[rank], dst.at[me], sends, recvs, base + 1 + k, device)
        copy.start()
        started.append(copy)
    return own, started


def exchange_wait(place, own, started, dst, sends, recvs, base):
    own.wait()
    for k, (device, rank) in enumerate(plane_peers(place)):
        spot = dst.at[rank]
        remote(spot, spot, sends, recvs, base + 1 + k, device).wait_recv()
    for copy in started:
        copy.wait_send()


PACK_ROWS = 16
HALF = 64


def prologue(w_qkv, tokens, pieces, lengths):
    heads_here = WIDTH // HD

    def body(qkv_ref, tok_ref, *refs):
        piece_refs, len_ref = refs[: len(pieces)], refs[len(pieces)]
        qkv_out, tok_out, vec_out, bias_out, len_out = refs[len(pieces) + 1 : len(pieces) + 6]
        packed, small, cut, sends, recvs, *swap = refs[len(pieces) + 6 :]
        place = Place()
        peers = plane_peers(place)
        others = z_peers(place)
        packed[...] = jnp.zeros_like(packed)
        for i, ref in enumerate(piece_refs):
            packed[i : i + 1, : ref.shape[1]] = ref[...].astype(jnp.float32)
        packed[8 : 8 + MB, :8] = len_ref[...].astype(jnp.float32)
        greet([device for device, _ in peers] + others, place)
        move = MoveIn(place, tok_ref, tok_out, *swap)
        move.start()
        me, z = place.rank, place.z
        own = pltpu.make_async_copy(packed, small.at[me, z], sends.at[1])
        own.start()
        first = []
        for j, device in enumerate(others):
            copy = remote(packed, small.at[me, z], sends, recvs, 2 + j, device)
            copy.start()
            first.append(copy)
        for p in range(8):
            columns = []
            for k in range(3):
                for at in range(heads_here):
                    lane = (k * HEADS + at * 8 + p) * HD
                    columns.append(qkv_ref[:, lane : lane + HD])
            cut[p] = jnp.concatenate(columns, axis=1)
        qkv = exchange_start(place, cut, qkv_out, sends, recvs, 16)
        move.middle()
        own.wait()
        for j, device in enumerate(others):
            spot = small.at[me, (z + Z - 1 - j) % Z]
            remote(spot, spot, sends, recvs, 2 + j, device).wait_recv()
        second = []
        for k, (device, rank) in enumerate(peers):
            copy = remote(small.at[me], small.at[me], sends, recvs, 8 + k, device)
            copy.start()
            second.append(copy)
        for k, (device, rank) in enumerate(peers):
            spot = small.at[rank]
            remote(spot, spot, sends, recvs, 8 + k, device).wait_recv()
        for at in range(Z):
            for p in range(0, 8, 2):
                both = [small[p, at, :8, :HALF], small[p + 1, at, :8, :HALF]]
                lane = (at * 8 + p) * HALF
                vec_out[:, lane : lane + 2 * HALF] = jnp.concatenate(both, axis=1)
        for k, row in enumerate((2, 6, 3)):
            for at in range(0, Z, 2):
                both = [small[me, at + j, row : row + 1, :HALF] for j in range(2)]
                lane = (k * Z + at) * HALF
                bias_out[:, lane : lane + 2 * HALF] = jnp.concatenate(both, axis=1)
        my_row = (z % 2) * 2 + z // 2
        len_out[...] = small[my_row, 0, 8 : 8 + MB, :8].astype(jnp.int32)
        for copy in first + second:
            copy.wait_send()
        exchange_wait(place, *qkv, qkv_out, sends, recvs, 16)
        move.finish()

    return kernel_call(
        body,
        (
            shape((8, w_qkv.shape[0], 3 * WIDTH)),
            shape(tokens.shape),
            shape((8, D), jnp.float32),
            shape((1, 3 * WIDTH), jnp.float32),
            shape((MB, 8), jnp.int32),
        ),
        [ANY_SPEC] * 2 + [VMEM_SPEC] * 3,
        [VMEM_SPEC, ANY_SPEC] + [VMEM_SPEC] * (len(pieces) + 1),
        [
            pltpu.VMEM((PACK_ROWS, 128), jnp.float32),
            pltpu.VMEM((8, Z, PACK_ROWS, 128), jnp.float32),
            pltpu.VMEM((8, w_qkv.shape[0], 3 * WIDTH), jnp.bfloat16),
            DMA((24,)),
            DMA((24,)),
        ]
        + MOVE_SCRATCH,
        0,
        (w_qkv, tokens, *pieces, lengths),
    )


def kernel_norm(values):
    average = jnp.mean(values, axis=-1, keepdims=True)
    centred = values - average
    inv_dev = lax.rsqrt(jnp.mean(centred * centred, axis=-1, keepdims=True) + NORM_EPS)
    return centred * inv_dev, inv_dev


FF_HERE = 704
FF_MAIN = 640
FF_BLOCK = 176


def first_gather(tokens, vectors, w_gate, w_up, cot):
    rows = w_gate.shape[0]

    def body(
        tok_ref, vec_ref, gate_ref, up_ref, cot_ref, one_out, gu_out, cot_out,
        own, cut, sends, recvs, gu_sends, gu_recvs, *swap,
    ):
        place = Place()
        for m in range(2):
            scaled, _ = kernel_norm(tok_ref[m].astype(jnp.float32))
            own[m] = (scaled * vec_ref[0:1, :] + vec_ref[1:2, :]).astype(jnp.bfloat16)
        greet([device for device, _ in plane_peers(place)], place)
        move = MoveIn(place, cot_ref, cot_out, *swap)
        move.start()
        steps = Gather(place, own, one_out, sends, recvs).steps()
        advance(steps)
        for p in range(8):

            def columns(ref):
                starts = [(at * 8 + p) * FF_BLOCK for at in range(Z)]
                return jnp.concatenate([ref[:, lane : lane + FF_BLOCK] for lane in starts], axis=1)

            gate, up = columns(gate_ref), columns(up_ref)
            cut[p, :, :FF_MAIN] = gate[:, :FF_MAIN]
            cut[p, :, FF_MAIN : 2 * FF_MAIN] = up[:, :FF_MAIN]
            cut[p, :, 2 * FF_MAIN :] = jnp.concatenate([gate[:, FF_MAIN:], up[:, FF_MAIN:]], axis=1)
        local, started = exchange_start(place, cut, gu_out, gu_sends, gu_recvs, 0)
        move.middle()
        for _ in steps:
            pass
        exchange_wait(place, local, started, gu_out, gu_sends, gu_recvs, 0)
        move.finish()

    return kernel_call(
        body,
        (shape(WHOLE + (D,)), shape((8, rows, 2 * FF_HERE)), shape(cot.shape)),
        [ANY_SPEC] * 3,
        [VMEM_SPEC] * 4 + [ANY_SPEC],
        [
            pltpu.VMEM((2, TOK, D), jnp.bfloat16),
            pltpu.VMEM((8, rows, 2 * FF_HERE), jnp.bfloat16),
            DMA((GATHER_SEMS,)),
            DMA((GATHER_SEMS,)),
            DMA((8,)),
            DMA((8,)),
        ]
        + MOVE_SCRATCH,
        1,
        (tokens, vectors, w_gate, w_up, cot),
    )


def out_projection(attended, row_out, tokens, vectors):
    def body(
        act_ref, weight_ref, tok_ref, vec_ref, res_out, two_out, own, sends, recvs, *scratch,
    ):
        place = Place()
        greet([place.px, place.py, place.ps])
        gather = Gather(place, own, two_out, sends, recvs)

        def finish(m, total):
            residual = tok_ref[m].astype(jnp.float32) + total
            res_out[m] = residual
            scaled, _ = kernel_norm(residual)
            own[m] = (scaled * vec_ref[4:5, :] + vec_ref[5:6, :]).astype(jnp.bfloat16)
            gather.send(m)

        plane_sum(place, act_ref, weight_ref, False, scratch, finish)
        gather.relay()
        gather.hand_over()
        gather.hand_over_far()
        gather.finish()

    return kernel_call(
        body,
        (shape((2, TOK, D), jnp.float32), shape(WHOLE + (D,))),
        [VMEM_SPEC, ANY_SPEC],
        [VMEM_SPEC] * 4,
        [
            pltpu.VMEM((2, TOK, D), jnp.bfloat16),
            DMA((GATHER_SEMS,)),
            DMA((GATHER_SEMS,)),
        ]
        + SUM_SCRATCH,
        2,
        (attended, row_out, tokens, vectors),
    )


def norm_grad(grad, scaled, inv_dev, gain):
    grad_scaled = grad * gain
    first_mean = jnp.mean(grad_scaled, axis=-1, keepdims=True)
    second_mean = jnp.mean(grad_scaled * scaled, axis=-1, keepdims=True)
    return inv_dev * (grad_scaled - first_mean - scaled * second_mean)


def ffn_backward(grad_gu, col_gu, residual, cot, vectors, hidden, row_down):
    def body(
        act_ref, weight_ref, res_in, cot_in, vec_ref, hidden_in, down_in,
        grad_out, branch_out, sums_out, parts_out,
        own, sends, recvs, staged, part_sems, res_ref, cot_ref, hidden_ref, down_ref, load_sems,
        *scratch,
    ):
        place = Place()
        pairs = ((hidden_in, hidden_ref), (down_in, down_ref), (res_in, res_ref), (cot_in, cot_ref))
        loads = [
            pltpu.make_async_copy(src, dst, load_sems.at[i]) for i, (src, dst) in enumerate(pairs)
        ]
        for load in loads:
            load.start()
        stores = []

        def part():
            i = len(stores)
            y, c, x = i // 4, i // 2 % 2, i % 2
            if i == 0:
                for load in loads:
                    load.wait()
            if i >= 2:
                stores[i - 2].wait()
            left = hidden_ref[y, c, :, x].reshape(2 * TOK, FF_HERE)

            def tile(j, _):
                cols = pl.ds(pl.multiple_of(j * COLUMNS, COLUMNS), COLUMNS)
                result = dot(left, down_ref[:, cols]).astype(jnp.bfloat16)
                staged[i % 2, :, :, cols] = result.reshape(2, TOK, COLUMNS)
                return 0

            lax.fori_loop(0, D // COLUMNS, tile, 0)
            copy = pltpu.make_async_copy(
                staged.at[i % 2], parts_out.at[y, c, :, x], part_sems.at[i % 2]
            )
            copy.start()
            stores.append(copy)

        def two_parts():
            part()
            part()

        greet([place.px, place.py, place.ps])
        gather = Gather(place, own, branch_out, sends, recvs)

        def finish(m, grad):
            scaled, inv_dev = kernel_norm(res_ref[m])
            result = cot_ref[m].astype(jnp.float32) + norm_grad(grad, scaled, inv_dev, vec_ref[4:5, :])
            grad_out[m] = result
            own[m] = result.astype(jnp.bfloat16)
            gather.send(m)
            by_gain = jnp.sum(grad * scaled, axis=0, keepdims=True)
            by_bias = jnp.sum(grad, axis=0, keepdims=True)
            if m == 0:
                sums_out[0:1, :] = by_gain
                sums_out[1:2, :] = by_bias
            else:
                sums_out[0:1, :] += by_gain
                sums_out[1:2, :] += by_bias

        plane_sum(place, act_ref, weight_ref, True, scratch, finish, two_parts)
        two_parts()
        gather.relay()
        two_parts()
        gather.hand_over()
        gather.hand_over_far()
        gather.finish()
        for copy in stores[-2:]:
            copy.wait()

    return kernel_call(
        body,
        (
            shape((2, TOK, D), jnp.float32),
            shape(WHOLE + (D,)),
            shape((2, D), jnp.float32),
            shape(WHOLE + (D,)),
        ),
        [VMEM_SPEC, ANY_SPEC, VMEM_SPEC, ANY_SPEC],
        [VMEM_SPEC] * 2 + [ANY_SPEC] * 2 + [VMEM_SPEC] + [ANY_SPEC] * 2,
        [
            pltpu.VMEM((2, TOK, D), jnp.bfloat16),
            DMA((GATHER_SEMS,)),
            DMA((GATHER_SEMS,)),
            pltpu.VMEM((2, 2, TOK, D), jnp.bfloat16),
            DMA((2,)),
            pltpu.VMEM((2, TOK, D), jnp.float32),
            pltpu.VMEM((2, TOK, D), jnp.bfloat16),
            pltpu.VMEM(hidden.shape, jnp.bfloat16),
            pltpu.VMEM(row_down.shape, jnp.bfloat16),
            DMA((4,)),
        ]
        + SUM_SCRATCH,
        3,
        (grad_gu, col_gu, residual, cot, vectors, hidden, row_down),
    )


def input_grad(
    grad_mixed, col_qkv, tokens, grad_residual, vectors, output, share_gu, sums_two, mixed_sums
):
    rows = share_gu.shape[1]
    heads_here = WIDTH // HD

    def body(
        act_ref, weight_ref, tok_ref, grad_ref, vec_ref, output_ref, gu_ref, two_ref, mixed_ref,
        own, packed, back_out, gate_out, up_out,
        sums_one, gu_in, gu_sends, gu_recvs, swap, move_sends, move_recvs, *scratch,
    ):
        place = Place()
        greet([device for device, _ in plane_peers(place)], place)
        move = MoveBack(place, output_ref, back_out, swap, move_sends, move_recvs)
        move.start()
        local, started = exchange_start(place, gu_ref, gu_in, gu_sends, gu_recvs, 0)

        def finish(m, grad):
            scaled, inv_dev = kernel_norm(tok_ref[m].astype(jnp.float32))
            result = grad_ref[m] + norm_grad(grad, scaled, inv_dev, vec_ref[0:1, :])
            own[m] = result.astype(jnp.bfloat16)
            by_gain = jnp.sum(grad * scaled, axis=0, keepdims=True)
            by_bias = jnp.sum(grad, axis=0, keepdims=True)
            if m == 0:
                sums_one[0:1, :] = by_gain
                sums_one[1:2, :] = by_bias
            else:
                sums_one[0:1, :] += by_gain
                sums_one[1:2, :] += by_bias

        stage = []

        def lay_out():
            stage.append(len(stage))
            if stage[-1] == 1:
                move.middle()
            if stage[-1] != 0:
                return
            packed[...] = jnp.zeros_like(packed)
            for at in range(Z):
                for p in range(8):
                    lane = (at * 8 + p) * HALF
                    packed[p, at, 4:6, :HALF] = two_ref[:, lane : lane + HALF]
            mixed = mixed_ref[0] + mixed_ref[1]
            for k, row in enumerate((2, 6, 3)):
                for at in range(heads_here):
                    lane = (k * heads_here + at) * HD
                    packed[place.rank, at, row : row + 1, :HALF] = mixed[:, lane : lane + HD]
            exchange_wait(place, local, started, gu_in, gu_sends, gu_recvs, 0)
            tail_at = 2 * FF_MAIN
            tail_mid = tail_at + FF_HERE - FF_MAIN
            gates, ups = [], []
            for p in range(8):
                block = gu_in[p].astype(jnp.float32)
                gates.append(
                    jnp.concatenate([block[:, :FF_MAIN], block[:, tail_at:tail_mid]], axis=1)
                )
                ups.append(jnp.concatenate([block[:, FF_MAIN:tail_at], block[:, tail_mid:]], axis=1))
            for out, blocks in ((gate_out, gates), (up_out, ups)):
                for at in range(Z):
                    lane = at * FF_BLOCK
                    pieces = [block[:, lane : lane + FF_BLOCK] for block in blocks]
                    joined = jnp.concatenate(pieces, axis=1).astype(jnp.bfloat16)
                    out[:, at * 8 * FF_BLOCK : (at + 1) * 8 * FF_BLOCK] = joined

        plane_sum(place, act_ref, weight_ref, True, scratch, finish, lay_out)
        for at in range(Z):
            for p in range(8):
                lane = (at * 8 + p) * HALF
                packed[p, at, 0:2, :HALF] = sums_one[:, lane : lane + HALF]
        move.finish()

    return kernel_call(
        body,
        (
            shape((2, TOK, D)),
            shape((8, Z, SMALL_ROWS, 128), jnp.float32),
            shape((2, TOK, D)),
            shape((rows, FF)),
            shape((rows, FF)),
        ),
        [VMEM_SPEC, VMEM_SPEC, ANY_SPEC, VMEM_SPEC, VMEM_SPEC],
        [VMEM_SPEC] * 5 + [ANY_SPEC] * 2 + [VMEM_SPEC] * 2,
        [
            pltpu.VMEM((2, D), jnp.float32),
            pltpu.VMEM(share_gu.shape, jnp.bfloat16),
            DMA((8,)),
            DMA((8,)),
        ]
        + MOVE_SCRATCH
        + SUM_SCRATCH,
        5,
        (
            grad_mixed, col_qkv, tokens, grad_residual, vectors, output, share_gu, sums_two, mixed_sums,
        ),
    )


SMALL_ROWS = 8


def epilogue(share_qkv, grad_tokens, packed):
    rows = share_qkv.shape[1]
    heads_here = WIDTH // HD

    def body(
        qkv_ref, tok_ref, packed_ref, qkv_out, tok_out, small_out,
        qkv_in, near, half, across, sends, recvs, *swap,
    ):
        place = Place()
        peers = plane_peers(place)
        others = z_peers(place)
        me = place.rank
        greet([device for device, _ in peers] + others, place)
        move = MoveBack(place, tok_ref, tok_out, *swap)
        move.start()
        qkv = exchange_start(place, qkv_ref, qkv_in, sends, recvs, 16)
        first = []
        for k, (device, rank) in enumerate(peers):
            copy = remote(packed_ref.at[rank], near.at[k], sends, recvs, 8 + k, device)
            copy.start()
            first.append(copy)
        added = packed_ref[me]
        for k, (device, rank) in enumerate(peers):
            spot = near.at[k]
            remote(spot, spot, sends, recvs, 8 + k, device).wait_recv()
            added = added + near[k]
        half[...] = added
        for j, device in enumerate(others):
            copy = remote(half.at[device[0]], across.at[j], sends, recvs, 2 + j, device)
            copy.start()
            first.append(copy)
        move.middle()
        exchange_wait(place, *qkv, qkv_in, sends, recvs, 16)
        for k in range(3):
            for at in range(heads_here):
                lane = (k * heads_here + at) * HD
                pieces = [qkv_in[p, :, lane : lane + HD].astype(jnp.float32) for p in range(8)]
                to = (k * HEADS + at * 8) * HD
                qkv_out[:, to : to + 8 * HD] = jnp.concatenate(pieces, axis=1)
        result = half[place.z]
        for j, device in enumerate(others):
            spot = across.at[j]
            remote(spot, spot, sends, recvs, 2 + j, device).wait_recv()
            result = result + across[j]
        small_out[...] = result
        for copy in first:
            copy.wait_send()
        move.finish()

    small = (SMALL_ROWS, 128)
    return kernel_call(
        body,
        (
            shape((rows, 3 * D), jnp.float32),
            shape(grad_tokens.shape),
            shape(small, jnp.float32),
        ),
        [VMEM_SPEC, ANY_SPEC, VMEM_SPEC],
        [ANY_SPEC] * 2 + [VMEM_SPEC],
        [
            pltpu.VMEM(share_qkv.shape, jnp.bfloat16),
            pltpu.VMEM((7, Z) + small, jnp.float32),
            pltpu.VMEM((Z,) + small, jnp.float32),
            pltpu.VMEM((Z - 1,) + small, jnp.float32),
            DMA((24,)),
            DMA((24,)),
        ]
        + MOVE_SCRATCH,
        6,
        (share_qkv, grad_tokens, packed),
    )


Q_BLOCK = 256
WIDTH = 256
SCALE = HD ** (-0.5)
PROJECTED = 512


def turn(values, cosine, sine, orient):
    lanes = lax.broadcasted_iota(jnp.int32, values.shape, 1) % HD
    lower = pltpu.roll(values, WIDTH - ROT // 2, 1)
    upper = pltpu.roll(values, ROT // 2, 1)
    swapped = jnp.where(lanes < ROT // 2, lower, upper)
    return values * cosine + orient * swapped * sine


def wide(table):
    return jnp.concatenate([table, table], axis=1)


def row_start(lengths_ref, m, first, rows=Q_BLOCK):
    queries = first + lax.broadcasted_iota(jnp.int32, (rows, 1), 0)
    start = jnp.zeros((rows, 1), jnp.int32)
    end = jnp.int32(0)
    for doc in range(8):
        end = end + lengths_ref[m, doc]
        start = jnp.where(queries >= end, end, start)
    return queries, start


def allowed_block(lengths_ref, m, first, keys):
    queries, start = row_start(lengths_ref, m, first)
    places = lax.broadcasted_iota(jnp.int32, (Q_BLOCK, keys), 1)
    return (places >= start) & (places <= queries)


def head_mask(h):
    lanes = lax.broadcasted_iota(jnp.int32, (1, WIDTH), 1)
    return (lanes // HD == h).astype(jnp.bfloat16)


def advance(steps):
    next(steps, None)


def attention_forward(all_one, col_qkv, bias, frequency, lengths, cot):
    row_len = all_one.shape[1]
    blocks = row_len // Q_BLOCK

    def body(
        len_ref, x_in, w_ref, bias_ref, freq_ref, cot_ref,
        q_out, k_out, v_out, att_out, lse_out, cos_ref, sin_ref, cot_out, sends, recvs,
        x_ref, load_sems,
    ):
        place = Place()
        loads = [pltpu.make_async_copy(x_in.at[m], x_ref.at[m], load_sems.at[m]) for m in range(MB)]
        for load in loads:
            load.start()
        greet([place.px, place.py, place.ps])
        steps = Gather(place, cot_ref, cot_out, sends, recvs).steps()
        advance(steps)
        lanes = lax.broadcasted_iota(jnp.int32, (Q_BLOCK, 128), 1)
        for m in range(MB):
            loads[m].wait()

            def project(i, _):
                first = pl.multiple_of(i * PROJECTED, PROJECTED)
                rows = pl.ds(first, PROJECTED)
                mixed = dot(x_ref[m, rows, :], w_ref[...]) + bias_ref[...]
                places, start = row_start(len_ref, m, first, PROJECTED)
                angles = (places - start).astype(jnp.float32) * freq_ref[...]
                cosine, sine = jnp.cos(angles), jnp.sin(angles)
                cos_ref[m, rows, :] = cosine
                sin_ref[m, rows, :] = sine
                cos_wide, sin_wide = wide(cosine), wide(sine)
                q_out[m, rows, :] = turn(mixed[:, :WIDTH], cos_wide, sin_wide, 1.0).astype(
                    jnp.bfloat16
                )
                k_out[m, rows, :] = turn(
                    mixed[:, WIDTH : 2 * WIDTH], cos_wide, sin_wide, 1.0
                ).astype(jnp.bfloat16)
                v_out[m, rows, :] = mixed[:, 2 * WIDTH :].astype(jnp.bfloat16)
                return 0

            lax.fori_loop(0, row_len // PROJECTED, project, 0)
            for i in range(blocks):
                first, keys = i * Q_BLOCK, (i + 1) * Q_BLOCK
                allowed = allowed_block(len_ref, m, first, keys)
                queries = q_out[m, first:keys, :]

                def head(h, carry):
                    summed, totals_all = carry
                    mask = head_mask(h)
                    scores = dot_last(queries * mask, k_out[m, :keys, :]) * SCALE
                    scores = jnp.where(allowed, scores, MASKED)
                    peak = jnp.max(scores, axis=-1, keepdims=True)
                    raised = jnp.exp(scores - peak)
                    totals = jnp.sum(raised, axis=-1, keepdims=True)
                    probs = (raised * (1.0 / totals)).astype(jnp.bfloat16)
                    by_head = dot(probs, v_out[m, :keys, :])
                    summed = summed + by_head * mask.astype(jnp.float32)
                    totals_all = jnp.where(lanes == h, peak + jnp.log(totals), totals_all)
                    return summed, totals_all

                summed, totals_all = lax.fori_loop(
                    0,
                    WIDTH // HD,
                    head,
                    (
                        jnp.zeros((Q_BLOCK, WIDTH), jnp.float32),
                        jnp.zeros((Q_BLOCK, 128), jnp.float32),
                    ),
                    unroll=2,
                )
                att_out[m, first:keys, :] = summed.astype(jnp.bfloat16)
                lse_out[m, first:keys, :] = totals_all
                if i % 2 == 1:
                    advance(steps)
        for _ in steps:
            pass

    return kernel_call(
        body,
        [shape((MB, row_len, WIDTH))] * 4
        + [shape((MB, row_len, 128), jnp.float32)] * 3
        + [shape(WHOLE + (D,))],
        [VMEM_SPEC] * 7 + [ANY_SPEC],
        [pl.BlockSpec(memory_space=pltpu.SMEM), ANY_SPEC] + [VMEM_SPEC] * 3 + [ANY_SPEC],
        [
            DMA((GATHER_SEMS,)),
            DMA((GATHER_SEMS,)),
            pltpu.VMEM(all_one.shape, jnp.bfloat16),
            DMA((MB,)),
        ],
        4,
        (lengths, all_one, col_qkv, bias, frequency, cot),
    )


def attention_backward(
    all_branch, row_out, queries, keys, values, lse, cosine, sine, lengths, parts, residual
):
    row_len = all_branch.shape[1]
    blocks = row_len // Q_BLOCK
    def body(
        len_ref, x_in, w_ref, q_ref, k_ref, v_ref, lse_ref, cos_ref, sin_ref, parts_ref,
        res_in, mixed_out, sums_out, own, grad_k, grad_v, grad_atts, x_ref, res_ref, load_sems,
        *scratch,
    ):
        place = Place()
        pairs = [(x_in.at[m], x_ref.at[m]) for m in range(MB)] + [(res_in, res_ref)]
        loads = [
            pltpu.make_async_copy(src, dst, load_sems.at[i]) for i, (src, dst) in enumerate(pairs)
        ]
        for load in loads:
            load.start()
        greet([place.px, place.py, place.ps])

        def store(m, total):
            own[m] = (res_ref[m] + total).astype(jnp.bfloat16)

        steps = sum_steps(place, parts_ref, store, scratch)
        advance(steps)
        lanes = lax.broadcasted_iota(jnp.int32, (Q_BLOCK, 128), 1)
        for m in range(MB):
            grad_k[...] = jnp.zeros_like(grad_k)
            grad_v[...] = jnp.zeros_like(grad_v)
            loads[m].wait()
            if m == 1:
                loads[2].wait()
            grad_atts[...] = dot_last(x_ref[m], w_ref[...]).astype(jnp.bfloat16)
            q_sum = jnp.zeros((1, WIDTH), jnp.float32)
            for i in range(blocks):
                first, count = i * Q_BLOCK, (i + 1) * Q_BLOCK
                allowed = allowed_block(len_ref, m, first, count)
                query_blk = q_ref[m, first:count, :]
                grad_att = grad_atts[first:count, :]
                totals_all = lse_ref[m, first:count, :]

                def head(h, grad_q):
                    mask = head_mask(h)
                    query_h, grad_h = query_blk * mask, grad_att * mask
                    totals = jnp.sum(
                        jnp.where(lanes == h, totals_all, 0.0), axis=-1, keepdims=True
                    )
                    scores = dot_last(query_h, k_ref[m, :count, :]) * SCALE
                    probs = jnp.where(allowed, jnp.exp(scores - totals), 0.0)
                    grad_probs = dot_last(grad_h, v_ref[m, :count, :])
                    inner = jnp.sum(probs * grad_probs, axis=-1, keepdims=True)
                    grad_scores = (probs * (grad_probs - inner)).astype(jnp.bfloat16)
                    grad_k[:count, :] += dot_first(grad_scores, query_h)
                    grad_v[:count, :] += dot_first(probs.astype(jnp.bfloat16), grad_h)
                    by_head = dot(grad_scores, k_ref[m, :count, :])
                    return grad_q + by_head * mask.astype(jnp.float32)

                grad_q = lax.fori_loop(
                    0, WIDTH // HD, head, jnp.zeros((Q_BLOCK, WIDTH), jnp.float32), unroll=2
                )
                cos_wide = wide(cos_ref[m, first:count, :])
                sin_wide = wide(sin_ref[m, first:count, :])
                grad_q = (grad_q * SCALE).astype(jnp.bfloat16).astype(jnp.float32)
                grad_q = turn(grad_q, cos_wide, sin_wide, -1.0).astype(jnp.bfloat16)
                mixed_out[m, first:count, :WIDTH] = grad_q
                q_sum = q_sum + jnp.sum(grad_q.astype(jnp.float32), axis=0, keepdims=True)
                if (m, i) in ((0, 0), (0, 2), (1, 3)):
                    advance(steps)
            k_sum = jnp.zeros((1, WIDTH), jnp.float32)
            v_sum = jnp.zeros((1, WIDTH), jnp.float32)
            for i in range(blocks):
                rows = slice(i * Q_BLOCK, (i + 1) * Q_BLOCK)
                cos_wide, sin_wide = wide(cos_ref[m, rows, :]), wide(sin_ref[m, rows, :])
                part = (grad_k[rows, :] * SCALE).astype(jnp.bfloat16).astype(jnp.float32)
                part = turn(part, cos_wide, sin_wide, -1.0).astype(jnp.bfloat16)
                mixed_out[m, rows, WIDTH : 2 * WIDTH] = part
                k_sum = k_sum + jnp.sum(part.astype(jnp.float32), axis=0, keepdims=True)
                part = grad_v[rows, :].astype(jnp.bfloat16)
                mixed_out[m, rows, 2 * WIDTH :] = part
                v_sum = v_sum + jnp.sum(part.astype(jnp.float32), axis=0, keepdims=True)
            sums_out[m] = jnp.concatenate([q_sum, k_sum, v_sum], axis=1)
        for _ in steps:
            pass

    return kernel_call(
        body,
        [
            shape((MB, row_len, 3 * WIDTH)),
            shape((MB, 1, 3 * WIDTH), jnp.float32),
            shape((MB, TOK, D)),
        ],
        [VMEM_SPEC] * 3,
        [pl.BlockSpec(memory_space=pltpu.SMEM), ANY_SPEC] + [VMEM_SPEC] * 7 + [ANY_SPEC] * 2,
        [
            pltpu.VMEM((row_len, WIDTH), jnp.float32),
            pltpu.VMEM((row_len, WIDTH), jnp.float32),
            pltpu.VMEM((row_len, WIDTH), jnp.bfloat16),
            pltpu.VMEM(all_branch.shape, jnp.bfloat16),
            pltpu.VMEM(residual.shape, jnp.float32),
            DMA((MB + 1,)),
        ]
        + STEP_SCRATCH,
        7,
        (
            lengths, all_branch, row_out, queries, keys, values, lse, cosine, sine, parts, residual,
        ),
    )


def sigmoid(values):
    return 1.0 / (1.0 + jnp.exp(-values))


def tail_parts(tail):
    lower = lax.broadcasted_iota(jnp.int32, tail.shape, 1) < 64
    rolled = pltpu.roll(tail, 64, 1)
    return lower, jnp.where(lower, tail, rolled), jnp.where(lower, rolled, tail)


def feed_forward(acts, col_gu):
    def body(x_ref, w_ref, gu_out, hidden_out):
        mixed = dot(x_ref[...], w_ref[...])
        gu_out[...] = mixed
        gate, up = mixed[:, :FF_MAIN], mixed[:, FF_MAIN : 2 * FF_MAIN]
        hidden_out[:, :FF_MAIN] = (gate * sigmoid(gate) * up).astype(jnp.bfloat16)
        _, gate, up = tail_parts(mixed[:, 2 * FF_MAIN :])
        tail = (gate * sigmoid(gate) * up).astype(jnp.bfloat16)
        hidden_out[:, FF_MAIN:] = tail[:, : FF_HERE - FF_MAIN]

    count = acts.shape[0]
    rows = 512
    return pl.pallas_call(
        body,
        out_shape=[shape((count, 2 * FF_HERE), jnp.float32), shape((count, FF_HERE))],
        grid=(count // rows,),
        in_specs=[
            pl.BlockSpec((rows, D), lambda i: (i, 0)),
            pl.BlockSpec((D, 2 * FF_HERE), lambda i: (0, 0)),
        ],
        out_specs=[
            pl.BlockSpec((rows, 2 * FF_HERE), lambda i: (i, 0)),
            pl.BlockSpec((rows, FF_HERE), lambda i: (i, 0)),
        ],
        cost_estimate=pl.CostEstimate(
            flops=4 * count * D * FF_HERE, bytes_accessed=30_000_000, transcendentals=0
        ),
        compiler_params=pltpu.CompilerParams(vmem_limit_bytes=VMEM_BYTES),
    )(acts, col_gu)


def feed_backward(cots, row_down, mixed):
    def body(cot_ref, w_ref, gu_ref, grad_out):
        grad = dot_last(cot_ref[...], w_ref[...])
        main = grad[:, :FF_MAIN]
        gate, up = gu_ref[:, :FF_MAIN], gu_ref[:, FF_MAIN : 2 * FF_MAIN]
        share = sigmoid(gate)
        silu = gate * share
        grad_out[:, :FF_MAIN] = (main * up * share * (1.0 + gate * (1.0 - share))).astype(
            jnp.bfloat16
        )
        grad_out[:, FF_MAIN : 2 * FF_MAIN] = (main * silu).astype(jnp.bfloat16)
        lower, gate, up = tail_parts(gu_ref[:, 2 * FF_MAIN :])
        tail = grad[:, FF_MAIN:]
        tail = jnp.concatenate([tail, tail], axis=1)
        share = sigmoid(gate)
        by_gate = tail * up * share * (1.0 + gate * (1.0 - share))
        by_up = tail * gate * share
        grad_out[:, 2 * FF_MAIN :] = jnp.where(lower, by_gate, by_up).astype(jnp.bfloat16)

    count = cots.shape[0]
    rows = 512
    return pl.pallas_call(
        body,
        out_shape=shape((count, 2 * FF_HERE)),
        grid=(count // rows,),
        in_specs=[
            pl.BlockSpec((rows, D), lambda i: (i, 0)),
            pl.BlockSpec((FF_HERE, D), lambda i: (0, 0)),
            pl.BlockSpec((rows, 2 * FF_HERE), lambda i: (i, 0)),
        ],
        out_specs=pl.BlockSpec((rows, 2 * FF_HERE), lambda i: (i, 0)),
        cost_estimate=pl.CostEstimate(
            flops=2 * count * D * FF_HERE, bytes_accessed=30_000_000, transcendentals=0
        ),
        compiler_params=pltpu.CompilerParams(vmem_limit_bytes=VMEM_BYTES),
    )(cots, row_down, mixed)


def local_fast(
    tokens,
    doc_lengths,
    ln1_gain,
    ln1_bias,
    w_qkv,
    q_bias,
    k_bias_rot,
    v_bias,
    w_out,
    ln2_gain,
    ln2_bias,
    w_gate,
    w_up,
    w_down,
    cotangent,
):
    plane = 8
    count = Z * plane
    z_at, x_at, y_at, c_at = (lax.axis_index(name) for name in ALL)
    rank = (x_at * 2 + y_at) * 2 + c_at
    row_len = N_TOK * TOK
    block = D // count
    rot_block = HEADS * ROT // count
    ff_block = FF // count
    heads_here = HEADS // plane
    ff_here = Z * ff_block
    every = MB * row_len

    tie = lax.optimization_barrier

    pieces = [ln1_gain, ln1_bias, q_bias, v_bias, ln2_gain, ln2_bias, k_bias_rot]
    pieces = [piece.reshape(1, -1) for piece in pieces]
    here_qkv, tok_here, vectors, bias_here, lengths = prologue(
        w_qkv, tokens[:, 0], pieces, doc_lengths[:, 0]
    )

    def over_z(array):
        return lax.all_gather(array, "z", axis=0, tiled=True)

    def sum_z(term):
        return lax.psum_scatter(term, "z", scatter_dimension=0, tiled=True)

    row_out = over_z(w_out)
    here_qkv, row_out = tie((here_qkv, row_out))
    col_qkv = over_z(here_qkv.reshape(plane * block, 3 * WIDTH))
    all_one, here_gu, cot_here = first_gather(tok_here, vectors, w_gate, w_up, cotangent[:, 0])
    here_gu, w_down = tie((here_gu, w_down))
    col_gu = over_z(here_gu.reshape(plane * block, 2 * ff_here))
    row_down = over_z(w_down)

    lane = jnp.arange(128, dtype=jnp.int32) % HD
    frequency = THETA ** (-2.0 * (lane % (ROT // 2)).astype(jnp.float32) / ROT)
    frequency = jnp.where(lane < ROT // 2, -frequency, jnp.where(lane < ROT, frequency, 0.0))

    queries, keys, values, attended, lse, cos_tab, sin_tab, all_cot = attention_forward(
        all_one.reshape(MB, row_len, D),
        col_qkv,
        bias_here,
        frequency.reshape(1, 128),
        lengths,
        cot_here,
    )
    residual, all_two = out_projection(
        attended.reshape(WHOLE + (WIDTH,)), row_out, tok_here, vectors
    )
    flat_one = all_one.reshape(every, D)
    flat_two = all_two.reshape(every, D)
    flat_cot = all_cot.reshape(every, D)

    def low(term):
        return term.astype(jnp.bfloat16)

    mixed_ff, hidden = feed_forward(flat_two, col_gu)
    term_down = low(dot_first(hidden, flat_cot))
    term_down, mixed_ff = tie((term_down, mixed_ff))
    share_down = sum_z(term_down)
    grad_gu = feed_backward(flat_cot, row_down, mixed_ff)
    term_gu = low(dot_first(flat_two, grad_gu))
    term_gu, grad_gu = tie((term_gu, grad_gu))
    share_gu = sum_z(term_gu).reshape(plane, block, 2 * ff_here)
    grad_residual, all_branch, sums_two, parts = ffn_backward(
        grad_gu.reshape(WHOLE + (2 * ff_here,)), col_gu, residual, cot_here, vectors,
        hidden.reshape(WHOLE + (ff_here,)), row_down,
    )
    term_out = low(dot_first(attended.reshape(every, WIDTH), all_branch.reshape(every, D)))
    term_out, all_branch, share_down = tie((term_out, all_branch, share_down))
    share_out = sum_z(term_out)
    grad_mixed, mixed_sums, output = attention_backward(
        all_branch.reshape(MB, row_len, D),
        row_out,
        queries,
        keys,
        values,
        lse,
        cos_tab,
        sin_tab,
        lengths,
        parts,
        residual,
    )
    term_qkv = low(dot_first(flat_one, grad_mixed.reshape(every, 3 * WIDTH)))
    term_qkv, grad_mixed, share_gu = tie((term_qkv, grad_mixed, share_gu))
    share_qkv = sum_z(term_qkv)
    grad_tokens, packed, output, share_gate, share_up = input_grad(
        grad_mixed.reshape(WHOLE + (3 * WIDTH,)),
        col_qkv,
        tok_here,
        grad_residual,
        vectors,
        output,
        share_gu,
        sums_two,
        mixed_sums,
    )
    share_down, share_out = share_down.astype(jnp.float32), share_out.astype(jnp.float32)
    share_gate, share_up = share_gate.astype(jnp.float32), share_up.astype(jnp.float32)
    packed, share_down, share_out, share_gate, share_up = tie(
        (packed, share_down, share_out, share_gate, share_up)
    )
    share_qkv, grad_tokens, shares = epilogue(
        share_qkv.reshape(plane, block, 3 * WIDTH), grad_tokens, packed
    )
    small_shares = [shares[i, :block] for i in (0, 1, 2, 3, 4, 5)]
    share_k = shares[6, :rot_block]
    return (
        output[:, None],
        grad_tokens[:, None],
        small_shares[0],
        small_shares[1],
        share_qkv,
        small_shares[2],
        share_k,
        small_shares[3],
        share_out,
        small_shares[4],
        small_shares[5],
        share_gate,
        share_up,
        share_down,
    )


def solution(mesh):
    xs = mesh.shape["seq"] // Z
    ys = mesh.shape["rows"] // 2
    fine = Mesh(mesh.devices.reshape(Z, xs, ys, 2), ALL)
    acts = P(None, ("y", "core"), ("z", "x"), None)
    vec = P(ALL)
    mat = P(ALL, None)
    small_plane = xs == 2 and ys == 2
    return jax.shard_map(
        local_fast if small_plane else local,
        mesh=fine,
        in_specs=(
            acts,
            P(None, ("y", "core"), None),
            vec,
            vec,
            mat,
            vec,
            vec,
            vec,
            mat,
            vec,
            vec,
            mat,
            mat,
            mat,
            acts,
        ),
        out_specs=(acts, acts, vec, vec, mat, vec, vec, vec, mat, vec, vec, mat, mat, mat),
        check_vma=False,
    )
```
